128 devices in a mesh: inp: 8 (over x, y_lo), tm: 16 (over y_hi, z, core).
Axes of the slice: x: 4, y: 4 (y_hi: 2, y_lo: 2; y = y_hi * 2 + y_lo), z: 4, core: 2. Of those that a mesh axis runs over, the one named last changes fastest.
Arguments:
- samples: int32 [512, 524288], P('inp', 'tm'), may hold values from -8 to 7
- filter_taps: int32 [4, 2048], replicated, may hold values from -4096 to 4095
Outputs:
- visibilities: float32 [2, 1024, 512, 512], P(None, ('inp', 'tm'))
The draws below stay inside these ranges and needn't reach their ends.
All inputs are finite; a program needn't handle non-finite values.
Results may differ from the reference program's by a relative error of at most 0.0032.
Values may be sent and summed in bfloat16 or wider, within the bound.
A program may use at most 128 MiB of HBM per device.

```python
import math
import jax
import jax.numpy as jnp
from jax import lax

NI = 512
FFT = 2048
TAPS = 4
CH = 1024
NSPEC = 256


def plant(array, rng, least, top_value):
    longest = array.shape.index(max(array.shape))
    spots = []
    for shift in (0, 1):
        where = [jax.random.randint(jax.random.fold_in(rng, axis), (), 0, length) for axis, length in enumerate(array.shape)]
        where[longest] = (where[longest] + shift) % array.shape[longest]
        spots.append(tuple(where))
    return array.at[spots[0]].set(least).at[spots[1]].set(top_value)


def setup_inputs(seed: int = 0) -> dict:
    streams_of = jax.random.split(jax.random.key(seed), 3)
    return {
        "samples": plant(jax.random.randint(streams_of[0], (NI, NSPEC * FFT), -8, 8), jax.random.fold_in(streams_of[0], 1), -8, 7).astype(jnp.int32),
        "filter_taps": plant(jax.random.randint(streams_of[1], (TAPS, FFT), -4096, 4096), jax.random.fold_in(streams_of[1], 1), -4096, 4095).astype(jnp.int32),
    }


def reference(samples, filter_taps):
    frames = samples.reshape(NI, NSPEC, FFT).astype(jnp.float32)
    padded = jnp.pad(frames, ((0, 0), (TAPS - 1, 0), (0, 0)))
    weights = filter_taps.astype(jnp.float32) / 16384.0
    filtered = jnp.zeros((NI, NSPEC, FFT), jnp.float32)
    for offset in range(TAPS):
        filtered = filtered + weights[offset] * padded[:, offset:offset + NSPEC, :]
    rounded = lax.optimization_barrier(filtered.astype(jnp.bfloat16)).astype(jnp.float32)
    spectrum = jnp.fft.rfft(rounded, axis=-1)[:, :, :CH] / math.sqrt(FFT)
    per_group = 8
    real_part = jnp.transpose(spectrum.real, (2, 0, 1)).reshape(CH // per_group, per_group, NI, NSPEC)
    imag_part = jnp.transpose(spectrum.imag, (2, 0, 1)).reshape(CH // per_group, per_group, NI, NSPEC)

    def correlate(pair):
        real_block, imag_block = pair
        highest = lax.Precision.HIGHEST
        power = jnp.einsum('cas,cbs->cab', real_block, real_block, precision=highest)
        power = power + jnp.einsum('cas,cbs->cab', imag_block, imag_block, precision=highest)
        phase = jnp.einsum('cas,cbs->cab', imag_block, real_block, precision=highest)
        phase = phase - jnp.einsum('cas,cbs->cab', real_block, imag_block, precision=highest)
        return jnp.stack([power, phase]) / NSPEC
    result = lax.map(correlate, (real_part, imag_part))
    return jnp.transpose(result, (1, 0, 2, 3, 4)).reshape(2, CH, NI, NI)
```

```python
import functools

import jax
import jax.numpy as jnp
import ml_dtypes
import numpy as np
from jax import lax
from jax.experimental import pallas as pl
from jax.experimental.pallas import tpu as pltpu
from jax.sharding import PartitionSpec as P

MESH = pl.DeviceIdType.MESH
LANES = 128
GROUP = 16
STRIDE = 53
VMEM = 60 * 2**20


def dft_table(frame_len, devices):
    channels = frame_len // 2
    points = np.arange(frame_len)
    turn = np.arange(channels)[:, None] * points[None, :] % frame_len
    wave = np.cos(2 * np.pi * points / frame_len)
    sine = np.sin(2 * np.pi * points / frame_len)
    rows = np.stack([wave[turn], -sine[turn]], axis=1)
    rows = rows.reshape(devices, 2 * channels // devices, frame_len)
    high = rows.astype(ml_dtypes.bfloat16)
    low = (rows - high.astype(np.float64)).astype(ml_dtypes.bfloat16)
    return np.stack([high, low])


def peer(step, total):
    inp, tm = lax.axis_index("inp"), lax.axis_index("tm")
    offset = (step * STRIDE) % total
    x = (inp // 2 + offset // 32) % 4
    y = ((tm // 8) * 2 + inp % 2 + (offset // 8) % 4) % 4
    z = ((tm // 2) % 4 + (offset // 2) % 4) % 4
    core = (tm + offset) % 2
    return x * 2 + y % 2, (y // 2) * 8 + z * 2 + core


def spectra_kernel(
    total,
    samples,
    taps,
    table,
    arrived,
    raw,
    past_out,
    past_in,
    filtered,
    tab,
    stage,
    outbox,
    raw_sem,
    tab_sem,
    past_sem,
    send_sem,
    recv_sem,
    own_sem,
):
    inputs = samples.shape[0]
    tap_count, frame_len = taps.shape
    spec_dev = samples.shape[1] // frame_len
    tm_count = lax.axis_size("tm")
    back = tap_count - 1
    half = spec_dev // 2
    rows = half * inputs
    inp, tm = lax.axis_index("inp"), lax.axis_index("tm")
    me = inp * tm_count + tm
    tiles = half * inputs // LANES
    msg = outbox.shape[2]

    def load(part, first, count):
        cut = pl.ds(first * frame_len, count * frame_len)
        return pltpu.make_async_copy(samples.at[:, cut], raw.at[:, cut], raw_sem.at[part])

    parts = [(spec_dev - back, back), (half - back, spec_dev - half), (0, half - back)]
    for part, (first, count) in enumerate(parts[:2]):
        load(part, first, count).start()

    def fetch(group):
        def one(k, carry):
            step = group * GROUP + k
            to_inp, to_tm = peer(step, total)
            pltpu.make_async_copy(
                table.at[:, to_inp * tm_count + to_tm], tab.at[:, step], tab_sem.at[group]
            ).start()
            return carry

        lax.fori_loop(0, GROUP, one, 0)

    fetch(0)
    load(2, *parts[2]).start()

    barrier = pltpu.get_barrier_semaphore()

    def greet(step, carry):
        pl.semaphore_signal(barrier, inc=1, device_id=peer(step, total), device_id_type=MESH)
        return carry

    lax.fori_loop(1, total, greet, 0)

    weights_of = lambda cut: [
        taps[k : k + 1, cut].astype(jnp.float32) for k in range(tap_count)
    ]

    def fir(first, count):
        def tile(n, carry):
            cut = pl.ds(pl.multiple_of(n * LANES, LANES), LANES)
            weights = weights_of(cut)

            def frame(s):
                if s < 0:
                    return past_in[(s + back) * inputs : (s + back + 1) * inputs, cut].astype(
                        jnp.float32
                    )
                at = pl.ds(pl.multiple_of(s * frame_len + n * LANES, LANES), LANES)
                return raw[:, at].astype(jnp.float32)

            window = [frame(first - back + k) for k in range(back)]
            for s in range(first, first + count):
                window.append(frame(s))
                value = weights[0] * window[0]
                for k in range(1, tap_count):
                    value = value + weights[k] * window[k]
                filtered[s * inputs : (s + 1) * inputs, cut] = value.astype(jnp.bfloat16)
                window.pop(0)
            return carry

        lax.fori_loop(0, frame_len // LANES, tile, 0)

    load(0, *parts[0]).wait()
    for k in range(back):
        first = (spec_dev - back + k) * frame_len
        past_out[k * inputs : (k + 1) * inputs, :] = (
            raw[:, first : first + frame_len].astype(jnp.float32).astype(jnp.bfloat16)
        )
    load(1, *parts[1]).wait()
    fir(half, half)

    pl.semaphore_wait(barrier, total - 1)
    past = pltpu.make_async_remote_copy(
        past_out,
        past_in,
        past_sem.at[0],
        past_sem.at[1],
        device_id=(inp, lax.rem(tm + 1, tm_count)),
        device_id_type=MESH,
    )

    @pl.when(tm < tm_count - 1)
    def _():
        past.start()

    for group in range(1, total // GROUP):
        fetch(group)

    def own(phase):
        return pltpu.make_async_copy(
            outbox.at[phase, 0], arrived.at[phase, me], own_sem.at[phase]
        )

    def channelize(phase, base):
        def group_step(group, carry):
            at = pl.ds(group * GROUP, GROUP)
            if phase == 0:
                pltpu.make_async_copy(tab.at[:, at], tab.at[:, at], tab_sem.at[group]).wait()
            frames = filtered[base : base + rows, :]
            value = None
            for part in range(2):
                lhs = tab[part, at].reshape(-1, frame_len)
                term = lax.dot_general(
                    lhs, frames, (((1,), (1,)), ((), ())), preferred_element_type=jnp.float32
                )
                value = term if value is None else value + term
            height = value.shape[0]
            for j in range(tiles):
                stage[pl.ds(j, height, stride=tiles), :] = value[:, j * LANES : (j + 1) * LANES]
            outbox[phase, at] = stage[...].reshape(GROUP, msg, LANES).astype(jnp.bfloat16)

            def send(k, carry):
                step = group * GROUP + k

                @pl.when(step == 0)
                def _():
                    own(phase).start()

                @pl.when(step > 0)
                def _():
                    pltpu.make_async_remote_copy(
                        outbox.at[phase, step],
                        arrived.at[phase, me],
                        send_sem.at[phase],
                        recv_sem.at[phase],
                        device_id=peer(step, total),
                        device_id_type=MESH,
                    ).start()

                return carry

            lax.fori_loop(0, GROUP, send, 0)
            return carry

        lax.fori_loop(0, total // GROUP, group_step, 0)

    channelize(0, rows)

    @pl.when(tm > 0)
    def _():
        pltpu.make_async_copy(past_in, past_in, past_sem.at[1]).wait()

    @pl.when(tm == 0)
    def _():
        past_in[...] = jnp.zeros_like(past_in)

    load(2, *parts[2]).wait()
    fir(0, half)
    channelize(1, 0)

    others = pl.ds(0, total - 1)
    for phase in range(2):
        own(phase).wait()
        sent, came = outbox.at[phase, others], arrived.at[phase, others]
        pltpu.make_async_copy(sent, sent, send_sem.at[phase]).wait()
        pltpu.make_async_copy(came, came, recv_sem.at[phase]).wait()

    @pl.when(tm < tm_count - 1)
    def _():
        pltpu.make_async_copy(past_out, past_out, past_sem.at[0]).wait()


def correlate_kernel(inputs, scale, arrived, out):
    phases, sources, rows, _ = arrived.shape
    pair = rows // 8
    lane_sets = LANES // inputs
    inp_count = out.shape[-1] // inputs
    times = sources // inp_count
    lane = lax.broadcasted_iota(jnp.int32, (1, 1, 1, LANES), 3)
    row = lax.broadcasted_iota(jnp.int32, (1, 1, 8, 1), 2)
    sign = jnp.where(row < 4, -1.0, 1.0).astype(jnp.float32)
    del lane_sets

    for c in range(pair):
        columns, turned = [], []
        for i in range(0, inp_count, 2):
            block = arrived[:, i * times : (i + 2) * times, :, :].astype(jnp.float32)
            block = block[:, :, c * 8 : (c + 1) * 8, :]
            even, odd = block[:, :times], block[:, times:]
            shape = even.shape
            flip = lambda v: pltpu.roll(v.reshape(-1, LANES), inputs, 1).reshape(shape)
            low = jnp.where(lane < inputs, even, flip(odd))
            high = jnp.where(lane < inputs, flip(even), odd)
            merged = jnp.concatenate([low, high], axis=0).reshape(-1, times, 8, LANES)
            swapped = jnp.concatenate([merged[:, :, 4:], merged[:, :, :4]], axis=2) * sign
            columns.append(merged.reshape(-1, LANES).astype(jnp.bfloat16))
            turned.append(swapped.reshape(-1, LANES).astype(jnp.bfloat16))
        spectra = jnp.concatenate(columns, axis=1)
        quarter = jnp.concatenate(turned, axis=1)
        across = spectra.T
        out[0, c] = jnp.dot(across, spectra, preferred_element_type=jnp.float32) * scale
        out[1, c] = jnp.dot(across, quarter, preferred_element_type=jnp.float32) * scale


def on_device(table, samples, filter_taps):
    inputs = samples.shape[0]
    tap_count, frame_len = filter_taps.shape
    spec_dev = samples.shape[1] // frame_len
    inp_count, tm_count = lax.axis_size("inp"), lax.axis_size("tm")
    total = inp_count * tm_count
    chan_dev = frame_len // 2 // total
    groups = total // GROUP
    tiles = spec_dev // 2 * inputs // LANES
    msg = 2 * chan_dev * tiles
    bf16 = jnp.bfloat16
    arrived = pl.pallas_call(
        functools.partial(spectra_kernel, total),
        out_shape=jax.ShapeDtypeStruct((2, total, msg, LANES), bf16),
        in_specs=[
            pl.BlockSpec(memory_space=pl.ANY),
            pl.BlockSpec(memory_space=pltpu.VMEM),
            pl.BlockSpec(memory_space=pl.ANY),
        ],
        out_specs=pl.BlockSpec(memory_space=pl.ANY),
        scratch_shapes=[
            pltpu.VMEM(samples.shape, jnp.int32),
            pltpu.VMEM(((tap_count - 1) * inputs, frame_len), bf16),
            pltpu.VMEM(((tap_count - 1) * inputs, frame_len), bf16),
            pltpu.VMEM((spec_dev * inputs, frame_len), bf16),
            pltpu.VMEM((2, total, 2 * chan_dev, frame_len), bf16),
            pltpu.VMEM((GROUP * msg, LANES), jnp.float32),
            pltpu.VMEM((2, total, msg, LANES), bf16),
            pltpu.SemaphoreType.DMA((3,)),
            pltpu.SemaphoreType.DMA((groups,)),
            pltpu.SemaphoreType.DMA((2,)),
            pltpu.SemaphoreType.DMA((2,)),
            pltpu.SemaphoreType.DMA((2,)),
            pltpu.SemaphoreType.DMA((2,)),
        ],
        compiler_params=pltpu.CompilerParams(
            collective_id=0, has_side_effects=True, vmem_limit_bytes=VMEM
        ),
        name="channelize_and_exchange",
    )(samples, filter_taps, table)

    scale = 1.0 / (16384.0**2 * frame_len * spec_dev * tm_count)
    all_inputs = inputs * inp_count
    pairs = chan_dev // 2
    return pl.pallas_call(
        functools.partial(correlate_kernel, inputs, scale),
        grid=(pairs,),
        out_shape=jax.ShapeDtypeStruct((2, chan_dev, all_inputs, all_inputs), jnp.float32),
        in_specs=[pl.BlockSpec((2, total, msg // pairs, LANES), lambda g: (0, 0, g, 0))],
        out_specs=pl.BlockSpec((2, 2, all_inputs, all_inputs), lambda g: (0, g, 0, 0)),
        compiler_params=pltpu.CompilerParams(vmem_limit_bytes=VMEM),
        name="correlate",
    )(arrived)


def solution(mesh):
    devices = mesh.size
    table = dft_table(2048, devices)

    def whole(samples, filter_taps):
        return jax.shard_map(
            on_device,
            mesh=mesh,
            in_specs=(P(), P("inp", "tm"), P()),
            out_specs=P(None, ("inp", "tm"), None, None),
            check_vma=False,
        )(jnp.asarray(table), samples, filter_taps)

    return whole
```

```python
import functools

import jax
import jax.numpy as jnp
import ml_dtypes
import numpy as np
from jax import lax
from jax.experimental import pallas as pl
from jax.experimental.pallas import tpu as pltpu
from jax.sharding import PartitionSpec as P

MESH = pl.DeviceIdType.MESH
LANES = 128
GROUP = 16
STRIDE = 11
PIECE = 32
VMEM = 60 * 2**20


def dft_table(frame_len, devices):
    channels = frame_len // 2
    points = np.arange(frame_len)
    turn = np.arange(channels)[:, None] * points[None, :] % frame_len
    wave = np.cos(2 * np.pi * points / frame_len)
    sine = np.sin(2 * np.pi * points / frame_len)
    rows = np.stack([wave[turn], -sine[turn]], axis=1)
    rows = rows.reshape(devices, 2 * channels // devices, frame_len)
    high = rows.astype(ml_dtypes.bfloat16)
    low = (rows - high.astype(np.float64)).astype(ml_dtypes.bfloat16)
    return np.stack([high, low])


def peer(step, total):
    inp, tm = lax.axis_index("inp"), lax.axis_index("tm")
    plane = total // 4
    rest = lax.max(step - plane, 0)
    far = step >= plane
    dz = jnp.where(far, 1 + lax.rem(rest, 3), 0)
    mixed = lax.rem(jnp.where(far, lax.div(rest, 3), step) * STRIDE, plane)
    x = lax.rem(lax.div(inp, 2) + lax.div(mixed, 8), 4)
    y = lax.rem(lax.div(tm, 8) * 2 + lax.rem(inp, 2) + lax.rem(lax.div(mixed, 2), 4), 4)
    z = lax.rem(lax.div(tm, 2) + dz, 4)
    core = lax.rem(tm + mixed, 2)
    return x * 2 + lax.rem(y, 2), lax.div(y, 2) * 8 + z * 2 + core


def spectra_kernel(
    total,
    samples,
    taps,
    table,
    arrived,
    raw,
    past_out,
    past_in,
    filtered,
    tab,
    stage,
    outbox,
    raw_sem,
    tab_sem,
    past_sem,
    send_sem,
    recv_sem,
    own_sem,
):
    inputs = samples.shape[0]
    tap_count, frame_len = taps.shape
    spec_dev = samples.shape[1] // frame_len
    tm_count = lax.axis_size("tm")
    back = tap_count - 1
    half = spec_dev // 2
    rows = half * inputs
    inp, tm = lax.axis_index("inp"), lax.axis_index("tm")
    me = inp * tm_count + tm
    tiles = half * inputs // LANES
    msg = outbox.shape[2]

    def load(part, first, count):
        cut = pl.ds(first * frame_len, count * frame_len)
        return pltpu.make_async_copy(samples.at[:, cut], raw.at[:, cut], raw_sem.at[part])

    parts = [(spec_dev - back, back), (half - back, spec_dev - half), (0, half - back)]
    for part, (first, count) in enumerate(parts[:2]):
        load(part, first, count).start()

    def fetch(group):
        def one(k, carry):
            step = group * GROUP + k
            to_inp, to_tm = peer(step, total)
            pltpu.make_async_copy(
                table.at[:, to_inp * tm_count + to_tm], tab.at[:, step], tab_sem.at[group]
            ).start()
            return carry

        lax.fori_loop(0, GROUP, one, 0)

    fetch(0)
    load(2, *parts[2]).start()

    barrier = pltpu.get_barrier_semaphore()

    def greet(step, carry):
        pl.semaphore_signal(barrier, inc=1, device_id=peer(step, total), device_id_type=MESH)
        return carry

    lax.fori_loop(1, total, greet, 0)

    weights_of = lambda cut: [
        taps[k : k + 1, cut].astype(jnp.float32) for k in range(tap_count)
    ]

    def fir(first, count):
        def tile(n, carry):
            cut = pl.ds(pl.multiple_of(n * LANES, LANES), LANES)
            weights = weights_of(cut)

            def frame(s):
                if s < 0:
                    return past_in[(s + back) * inputs : (s + back + 1) * inputs, cut].astype(
                        jnp.float32
                    )
                at = pl.ds(pl.multiple_of(s * frame_len + n * LANES, LANES), LANES)
                return raw[:, at].astype(jnp.float32)

            window = [frame(first - back + k) for k in range(back)]
            for s in range(first, first + count):
                window.append(frame(s))
                value = weights[0] * window[0]
                for k in range(1, tap_count):
                    value = value + weights[k] * window[k]
                filtered[s * inputs : (s + 1) * inputs, cut] = value.astype(jnp.bfloat16)
                window.pop(0)
            return carry

        lax.fori_loop(0, frame_len // LANES, tile, 0)

    load(0, *parts[0]).wait()
    for k in range(back):
        first = (spec_dev - back + k) * frame_len
        past_out[k * inputs : (k + 1) * inputs, :] = (
            raw[:, first : first + frame_len].astype(jnp.float32).astype(jnp.bfloat16)
        )
    def hand_on(piece):
        cut = pl.ds(piece * PIECE, PIECE)
        return pltpu.make_async_remote_copy(
            past_out.at[cut],
            past_in.at[cut],
            past_sem.at[0],
            past_sem.at[1],
            device_id=(inp, lax.rem(tm + 1, tm_count)),
            device_id_type=MESH,
        )

    pl.semaphore_wait(barrier, total - 1)

    @pl.when(tm < tm_count - 1)
    def _():
        for piece in range(back * inputs // PIECE):
            hand_on(piece).start()

    load(1, *parts[1]).wait()
    fir(half, half)

    for group in range(1, total // GROUP):
        fetch(group)

    def own(phase):
        return pltpu.make_async_copy(
            outbox.at[phase, 0], arrived.at[phase, me], own_sem.at[phase]
        )

    def channelize(phase, base):
        def group_step(group, carry):
            at = pl.ds(group * GROUP, GROUP)
            if phase == 0:
                pltpu.make_async_copy(tab.at[:, at], tab.at[:, at], tab_sem.at[group]).wait()
            frames = filtered[base : base + rows, :]
            value = None
            for part in range(2):
                lhs = tab[part, at].reshape(-1, frame_len)
                term = lax.dot_general(
                    lhs, frames, (((1,), (1,)), ((), ())), preferred_element_type=jnp.float32
                )
                value = term if value is None else value + term
            height = value.shape[0]
            for j in range(tiles):
                stage[pl.ds(j, height, stride=tiles), :] = value[:, j * LANES : (j + 1) * LANES]
            outbox[phase, at] = stage[...].reshape(GROUP, msg, LANES).astype(jnp.bfloat16)

            def send(k, carry):
                step = group * GROUP + k

                @pl.when(step == 0)
                def _():
                    own(phase).start()

                @pl.when(step > 0)
                def _():
                    pltpu.make_async_remote_copy(
                        outbox.at[phase, step],
                        arrived.at[phase, me],
                        send_sem.at[phase],
                        recv_sem.at[phase],
                        device_id=peer(step, total),
                        device_id_type=MESH,
                    ).start()

                return carry

            lax.fori_loop(0, GROUP, send, 0)
            return carry

        lax.fori_loop(0, total // GROUP, group_step, 0)

    channelize(0, rows)

    @pl.when(tm > 0)
    def _():
        pltpu.make_async_copy(past_in, past_in, past_sem.at[1]).wait()

    @pl.when(tm == 0)
    def _():
        past_in[...] = jnp.zeros_like(past_in)

    load(2, *parts[2]).wait()
    fir(0, half)
    channelize(1, 0)

    others = pl.ds(0, total - 1)
    for phase in range(2):
        own(phase).wait()
        sent, came = outbox.at[phase, others], arrived.at[phase, others]
        pltpu.make_async_copy(sent, sent, send_sem.at[phase]).wait()
        pltpu.make_async_copy(came, came, recv_sem.at[phase]).wait()

    @pl.when(tm < tm_count - 1)
    def _():
        pltpu.make_async_copy(past_out, past_out, past_sem.at[0]).wait()


def correlate_kernel(inputs, scale, arrived, out):
    phases, sources, rows, _ = arrived.shape
    pair = rows // 8
    lane_sets = LANES // inputs
    inp_count = out.shape[-1] // inputs
    times = sources // inp_count
    lane = lax.broadcasted_iota(jnp.int32, (1, 1, 1, LANES), 3)
    row = lax.broadcasted_iota(jnp.int32, (1, 1, 8, 1), 2)
    sign = jnp.where(row < 4, -1.0, 1.0).astype(jnp.float32)
    del lane_sets

    for c in range(pair):
        columns, turned = [], []
        for i in range(0, inp_count, 2):
            block = arrived[:, i * times : (i + 2) * times, :, :].astype(jnp.float32)
            block = block[:, :, c * 8 : (c + 1) * 8, :]
            even, odd = block[:, :times], block[:, times:]
            shape = even.shape
            flip = lambda v: pltpu.roll(v.reshape(-1, LANES), inputs, 1).reshape(shape)
            low = jnp.where(lane < inputs, even, flip(odd))
            high = jnp.where(lane < inputs, flip(even), odd)
            merged = jnp.concatenate([low, high], axis=0).reshape(-1, times, 8, LANES)
            swapped = jnp.concatenate([merged[:, :, 4:], merged[:, :, :4]], axis=2) * sign
            columns.append(merged.reshape(-1, LANES).astype(jnp.bfloat16))
            turned.append(swapped.reshape(-1, LANES).astype(jnp.bfloat16))
        spectra = jnp.concatenate(columns, axis=1)
        quarter = jnp.concatenate(turned, axis=1)
        across = spectra.T
        out[0, c] = jnp.dot(across, spectra, preferred_element_type=jnp.float32) * scale
        out[1, c] = jnp.dot(across, quarter, preferred_element_type=jnp.float32) * scale


def on_device(table, samples, filter_taps):
    inputs = samples.shape[0]
    tap_count, frame_len = filter_taps.shape
    spec_dev = samples.shape[1] // frame_len
    inp_count, tm_count = lax.axis_size("inp"), lax.axis_size("tm")
    total = inp_count * tm_count
    chan_dev = frame_len // 2 // total
    groups = total // GROUP
    tiles = spec_dev // 2 * inputs // LANES
    msg = 2 * chan_dev * tiles
    bf16 = jnp.bfloat16
    arrived = pl.pallas_call(
        functools.partial(spectra_kernel, total),
        out_shape=jax.ShapeDtypeStruct((2, total, msg, LANES), bf16),
        in_specs=[
            pl.BlockSpec(memory_space=pl.ANY),
            pl.BlockSpec(memory_space=pltpu.VMEM),
            pl.BlockSpec(memory_space=pl.ANY),
        ],
        out_specs=pl.BlockSpec(memory_space=pl.ANY),
        scratch_shapes=[
            pltpu.VMEM(samples.shape, jnp.int32),
            pltpu.VMEM(((tap_count - 1) * inputs, frame_len), bf16),
            pltpu.VMEM(((tap_count - 1) * inputs, frame_len), bf16),
            pltpu.VMEM((spec_dev * inputs, frame_len), bf16),
            pltpu.VMEM((2, total, 2 * chan_dev, frame_len), bf16),
            pltpu.VMEM((GROUP * msg, LANES), jnp.float32),
            pltpu.VMEM((2, total, msg, LANES), bf16),
            pltpu.SemaphoreType.DMA((3,)),
            pltpu.SemaphoreType.DMA((groups,)),
            pltpu.SemaphoreType.DMA((2,)),
            pltpu.SemaphoreType.DMA((2,)),
            pltpu.SemaphoreType.DMA((2,)),
            pltpu.SemaphoreType.DMA((2,)),
        ],
        compiler_params=pltpu.CompilerParams(
            collective_id=0, has_side_effects=True, vmem_limit_bytes=VMEM
        ),
        name="channelize_and_exchange",
    )(samples, filter_taps, table)

    scale = 1.0 / (16384.0**2 * frame_len * spec_dev * tm_count)
    all_inputs = inputs * inp_count
    pairs = chan_dev // 2
    return pl.pallas_call(
        functools.partial(correlate_kernel, inputs, scale),
        grid=(pairs,),
        out_shape=jax.ShapeDtypeStruct((2, chan_dev, all_inputs, all_inputs), jnp.float32),
        in_specs=[pl.BlockSpec((2, total, msg // pairs, LANES), lambda g: (0, 0, g, 0))],
        out_specs=pl.BlockSpec((2, 2, all_inputs, all_inputs), lambda g: (0, g, 0, 0)),
        compiler_params=pltpu.CompilerParams(vmem_limit_bytes=VMEM),
        name="correlate",
    )(arrived)


def solution(mesh):
    devices = mesh.size
    table = dft_table(2048, devices)

    def whole(samples, filter_taps):
        return jax.shard_map(
            on_device,
            mesh=mesh,
            in_specs=(P(), P("inp", "tm"), P()),
            out_specs=P(None, ("inp", "tm"), None, None),
            check_vma=False,
        )(jnp.asarray(table), samples, filter_taps)

    return whole
```

```python
import functools

import jax
import jax.numpy as jnp
import ml_dtypes
import numpy as np
from jax import lax
from jax.experimental import pallas as pl
from jax.experimental.pallas import tpu as pltpu
from jax.sharding import PartitionSpec as P

MESH = pl.DeviceIdType.MESH
LANES = 128
QUAD = 4
GROUP = 16
STRIDE = 11
PIECE = 32
VMEM = 44 * 2**20


def dft_table(frame_len, devices):
    channels = frame_len // 2
    points = np.arange(frame_len)
    turn = np.arange(channels)[:, None] * points[None, :] % frame_len
    wave = np.cos(2 * np.pi * points / frame_len)
    sine = np.sin(2 * np.pi * points / frame_len)
    rows = np.stack([wave[turn], -sine[turn]])
    high = rows.astype(ml_dtypes.bfloat16)
    low = (rows - high.astype(np.float64)).astype(ml_dtypes.bfloat16)
    parts = np.stack([high, low]).reshape(2, 2, devices, 2, QUAD, frame_len)
    return parts.transpose(3, 2, 0, 1, 4, 5).reshape(2, devices, 4 * QUAD, frame_len)


def peer(step, total):
    inp, tm = lax.axis_index("inp"), lax.axis_index("tm")
    plane = total // 4
    rest = lax.max(step - plane, 0)
    far = step >= plane
    dz = jnp.where(far, 1 + lax.rem(rest, 3), 0)
    mixed = lax.rem(jnp.where(far, lax.div(rest, 3), step) * STRIDE, plane)
    x = lax.rem(lax.div(inp, 2) + lax.div(mixed, 8), 4)
    y = lax.rem(lax.div(tm, 8) * 2 + lax.rem(inp, 2) + lax.rem(lax.div(mixed, 2), 4), 4)
    z = lax.rem(lax.div(tm, 2) + dz, 4)
    core = lax.rem(tm + mixed, 2)
    return x * 2 + lax.rem(y, 2), lax.div(y, 2) * 8 + z * 2 + core


def interleave(value):
    sets = [value[:, :, j * LANES : (j + 1) * LANES] for j in range(QUAD)]
    row = lax.broadcasted_iota(jnp.int32, (1, 8, 1), 1)

    def exchange(first, second, reach):
        keep = lax.rem(lax.div(row, reach), 2) == 0
        low = jnp.where(keep, first, pltpu.roll(second, reach, 1))
        high = jnp.where(keep, pltpu.roll(first, 8 - reach, 1), second)
        return low, high

    near, far = zip(exchange(sets[0], sets[2], 2), exchange(sets[1], sets[3], 2))
    near, far = (near[0], far[0]), (near[1], far[1])
    channels = [*exchange(near[0], far[0], 1), *exchange(near[1], far[1], 1)]
    return jnp.concatenate(channels, axis=1)


def correlate(first, second, scale, vis, at):
    all_inputs = vis.shape[-1]
    sources = first.shape[0]
    inputs = LANES // 2
    inp_count = all_inputs // inputs
    times = sources // inp_count
    lane = lax.broadcasted_iota(jnp.int32, (1, 1, LANES), 2)
    row = lax.broadcasted_iota(jnp.int32, (1, 8, 1), 1)
    sign = jnp.where(row < QUAD, -1.0, 1.0).astype(jnp.float32)
    for c in range(2):
        columns, turned = [], []
        for i in range(0, inp_count, 2):
            low, high = [], []
            for ref in (first, second):
                block = ref[i * times : (i + 2) * times].astype(jnp.float32)
                block = block[:, c * 8 : (c + 1) * 8, :]
                even, odd = block[:times], block[times:]
                low.append(jnp.where(lane < inputs, even, pltpu.roll(odd, inputs, 2)))
                high.append(jnp.where(lane < inputs, pltpu.roll(even, inputs, 2), odd))
            merged = jnp.concatenate(low + high, axis=0)
            swapped = pltpu.roll(merged, QUAD, 1) * sign
            columns.append(merged.reshape(-1, LANES).astype(jnp.bfloat16))
            turned.append(swapped.reshape(-1, LANES).astype(jnp.bfloat16))
        spectra = jnp.concatenate(columns, axis=1)
        quarter = jnp.concatenate(turned, axis=1)
        across = spectra.T
        vis[0, at + c] = jnp.dot(across, spectra, preferred_element_type=jnp.float32) * scale
        vis[1, at + c] = jnp.dot(across, quarter, preferred_element_type=jnp.float32) * scale


def correlate_half(half, early, late, scale, vis, done=None):
    def pair(k, carry):
        rows = pl.ds(pl.multiple_of(k * 16, 16), 16)
        early_rows = pl.ds(pl.multiple_of(half * 8 * QUAD + k * 16, 16), 16)
        correlate(early.at[:, early_rows], late.at[half, :, rows], scale, vis, 2 * k)
        if done is not None:
            done(k)
        return carry

    lax.fori_loop(0, QUAD // 2, pair, 0)


def spectra_kernel(
    total,
    scale,
    samples,
    taps,
    table,
    early,
    late,
    vis,
    raw,
    past_out,
    past_in,
    filtered,
    tab,
    early_box,
    late_box,
    raw_sem,
    tab_sem,
    past_sem,
    send_sem,
    recv_sem,
    own_sem,
):
    inputs = samples.shape[0]
    tap_count, frame_len = taps.shape
    spec_dev = samples.shape[1] // frame_len
    tm_count = lax.axis_size("tm")
    back = tap_count - 1
    half = spec_dev // 2
    rows = half * inputs
    inp, tm = lax.axis_index("inp"), lax.axis_index("tm")
    me = inp * tm_count + tm
    groups = total // GROUP

    def load(part, first, count):
        cut = pl.ds(first * frame_len, count * frame_len)
        return pltpu.make_async_copy(samples.at[:, cut], raw.at[:, cut], raw_sem.at[part])

    parts = [(spec_dev - back, back), (half - back, spec_dev - half), (0, half - back)]
    for part, (first, count) in enumerate(parts[:2]):
        load(part, first, count).start()

    def fetch(group):
        def one(k, carry):
            step = group * GROUP + k
            to_inp, to_tm = peer(step, total)
            pltpu.make_async_copy(
                table.at[:, to_inp * tm_count + to_tm], tab.at[:, step], tab_sem.at[group]
            ).start()
            return carry

        lax.fori_loop(0, GROUP, one, 0)

    fetch(0)
    load(2, *parts[2]).start()

    barrier = pltpu.get_barrier_semaphore()

    def greet(step, carry):
        pl.semaphore_signal(barrier, inc=1, device_id=peer(step, total), device_id_type=MESH)
        return carry

    lax.fori_loop(1, total, greet, 0)

    weights_of = lambda cut: [
        taps[k : k + 1, cut].astype(jnp.float32) for k in range(tap_count)
    ]

    def fir(first, count):
        def tile(n, carry):
            cut = pl.ds(pl.multiple_of(n * LANES, LANES), LANES)
            weights = weights_of(cut)

            def frame(s):
                if s < 0:
                    return past_in[(s + back) * inputs : (s + back + 1) * inputs, cut].astype(
                        jnp.float32
                    )
                at = pl.ds(pl.multiple_of(s * frame_len + n * LANES, LANES), LANES)
                return raw[:, at].astype(jnp.float32)

            window = [frame(first - back + k) for k in range(back)]
            for s in range(first, first + count):
                window.append(frame(s))
                value = weights[0] * window[0]
                for k in range(1, tap_count):
                    value = value + weights[k] * window[k]
                filtered[s * inputs : (s + 1) * inputs, cut] = value.astype(jnp.bfloat16)
                window.pop(0)
            return carry

        lax.fori_loop(0, frame_len // LANES, tile, 0)

    load(0, *parts[0]).wait()
    for k in range(back):
        first = (spec_dev - back + k) * frame_len
        past_out[k * inputs : (k + 1) * inputs, :] = (
            raw[:, first : first + frame_len].astype(jnp.float32).astype(jnp.bfloat16)
        )
    def hand_on(piece):
        cut = pl.ds(piece * PIECE, PIECE)
        return pltpu.make_async_remote_copy(
            past_out.at[cut],
            past_in.at[cut],
            past_sem.at[0],
            past_sem.at[1],
            device_id=(inp, lax.rem(tm + 1, tm_count)),
            device_id_type=MESH,
        )

    pl.semaphore_wait(barrier, total - 1)

    @pl.when(tm < tm_count - 1)
    def _():
        for piece in range(back * inputs // PIECE):
            hand_on(piece).start()

    load(1, *parts[1]).wait()
    fir(half, half)

    boxes = [
        (lambda step: early_box.at[step], lambda: early.at[me], early_box, early),
        (lambda step: late_box.at[0, step], lambda: late.at[0, me], late_box.at[0], late.at[0]),
        (lambda step: late_box.at[1, step], lambda: late.at[1, me], late_box.at[1], late.at[1]),
    ]

    def own(phase):
        source, target = boxes[phase][:2]
        return pltpu.make_async_copy(source(0), target(), own_sem.at[phase])

    def channelize(phase, base, halves):
        source, target = boxes[phase][:2]

        def group_step(index, carry):
            group = index if phase == 0 else lax.rem(index * 3 + 2, groups)
            at = pl.ds(group * GROUP, GROUP)
            if phase == 0:

                pltpu.make_async_copy(tab.at[:, at], tab.at[:, at], tab_sem.at[group]).wait()
            frames = filtered[base : base + rows, :]
            for h in halves:
                value = lax.dot_general(
                    tab[h, at].reshape(-1, frame_len),
                    frames,
                    (((1,), (1,)), ((), ())),
                    preferred_element_type=jnp.float32,
                ).reshape(GROUP, 2, 2 * QUAD, -1)
                box = interleave(value[:, 0] + value[:, 1]).astype(jnp.bfloat16)
                if phase == 0:
                    early_box[at, h * 8 * QUAD : (h + 1) * 8 * QUAD] = box
                else:
                    late_box[h, at] = box

            def send(k, carry):
                step = group * GROUP + k

                @pl.when(step == 0)
                def _():
                    own(phase).start()

                @pl.when(step > 0)
                def _():
                    pltpu.make_async_remote_copy(
                        source(step),
                        target(),
                        send_sem.at[phase],
                        recv_sem.at[phase],
                        device_id=peer(step, total),
                        device_id_type=MESH,
                    ).start()

                return carry

            lax.fori_loop(0, GROUP, send, 0)
            return carry

        lax.fori_loop(0, groups, group_step, 0)

    for g in range(1, groups):
        fetch(g)
    channelize(0, rows, (0, 1))

    @pl.when(tm > 0)
    def _():
        pltpu.make_async_copy(past_in, past_in, past_sem.at[1]).wait()

    @pl.when(tm == 0)
    def _():
        past_in[...] = jnp.zeros_like(past_in)

    load(2, *parts[2]).wait()
    fir(0, half)
    channelize(1, 0, (0,))
    channelize(2, 0, (1,))

    others = pl.ds(0, total - 1)

    def arrive(phase):
        came = boxes[phase][3].at[others]
        own(phase).wait()
        pltpu.make_async_copy(came, came, recv_sem.at[phase]).wait()

    arrive(0)
    arrive(1)
    correlate_half(0, early, late, scale, vis)
    arrive(2)
    for phase in range(3):
        sent = boxes[phase][2].at[others]
        pltpu.make_async_copy(sent, sent, send_sem.at[phase]).wait()

    @pl.when(tm < tm_count - 1)
    def _():
        pltpu.make_async_copy(past_out, past_out, past_sem.at[0]).wait()


def correlate_kernel(scale, early, late, vis, out, rest, sem):
    def write(source, k, first):
        pair = pl.ds(2 * k, 2)
        return pltpu.make_async_copy(source.at[:, pair], out.at[:, pl.ds(first + 2 * k, 2)], sem)

    def begin(k, carry):
        write(vis, k, 0).start()
        return carry

    lax.fori_loop(0, QUAD // 2, begin, 0)
    correlate_half(1, early, late, scale, rest, lambda k: write(rest, k, QUAD).start())
    pltpu.make_async_copy(out, out, sem).wait()


def on_device(table, samples, filter_taps):
    inputs = samples.shape[0]
    tap_count, frame_len = filter_taps.shape
    spec_dev = samples.shape[1] // frame_len
    inp_count, tm_count = lax.axis_size("inp"), lax.axis_size("tm")
    total = inp_count * tm_count
    chan_dev = frame_len // 2 // total
    groups = total // GROUP
    all_inputs = inputs * inp_count
    bf16 = jnp.bfloat16
    scale = 1.0 / (16384.0**2 * frame_len * spec_dev * tm_count)
    early_shape = (total, 16 * QUAD, LANES)
    late_shape = (2, total, 8 * QUAD, LANES)
    vis_shape = (2, QUAD, all_inputs, all_inputs)
    hbm = pl.BlockSpec(memory_space=pltpu.HBM)
    vmem = pl.BlockSpec(memory_space=pltpu.VMEM)
    early, late, vis = pl.pallas_call(
        functools.partial(spectra_kernel, total, scale),
        out_shape=[
            pltpu.VMEM(early_shape, bf16),
            pltpu.VMEM(late_shape, bf16),
            pltpu.VMEM(vis_shape, jnp.float32),
        ],
        in_specs=[hbm, vmem, hbm],
        out_specs=[vmem, vmem, vmem],
        scratch_shapes=[
            pltpu.VMEM(samples.shape, jnp.int32),
            pltpu.VMEM(((tap_count - 1) * inputs, frame_len), bf16),
            pltpu.VMEM(((tap_count - 1) * inputs, frame_len), bf16),
            pltpu.VMEM((spec_dev * inputs, frame_len), bf16),
            pltpu.VMEM((2, total, 4 * QUAD, frame_len), bf16),
            pltpu.VMEM(early_shape, bf16),
            pltpu.VMEM(late_shape, bf16),
            pltpu.SemaphoreType.DMA((3,)),
            pltpu.SemaphoreType.DMA((groups,)),
            pltpu.SemaphoreType.DMA((2,)),
            pltpu.SemaphoreType.DMA((3,)),
            pltpu.SemaphoreType.DMA((3,)),
            pltpu.SemaphoreType.DMA((3,)),
        ],
        compiler_params=pltpu.CompilerParams(
            collective_id=0, has_side_effects=True, vmem_limit_bytes=VMEM
        ),
        name="channelize_and_exchange",
    )(samples, filter_taps, table)
    return pl.pallas_call(
        functools.partial(correlate_kernel, scale),
        out_shape=jax.ShapeDtypeStruct((2, chan_dev, all_inputs, all_inputs), jnp.float32),
        in_specs=[vmem, vmem, vmem],
        out_specs=hbm,
        scratch_shapes=[pltpu.VMEM(vis_shape, jnp.float32), pltpu.SemaphoreType.DMA],
        compiler_params=pltpu.CompilerParams(vmem_limit_bytes=VMEM // 2),
        name="correlate",
    )(early, late, vis)


def solution(mesh):
    devices = mesh.size
    table = dft_table(2048, devices)

    def whole(samples, filter_taps):
        return jax.shard_map(
            on_device,
            mesh=mesh,
            in_specs=(P(), P("inp", "tm"), P()),
            out_specs=P(None, ("inp", "tm"), None, None),
            check_vma=False,
        )(jnp.asarray(table), samples, filter_taps)

    return whole
```

```python
import functools

import jax
import jax.numpy as jnp
import ml_dtypes
import numpy as np
from jax import lax
from jax.experimental import pallas as pl
from jax.experimental.pallas import tpu as pltpu
from jax.sharding import PartitionSpec as P

MESH = pl.DeviceIdType.MESH
LANES = 128
QUAD = 4
GROUP = 16
STRIDE = 5
AHEAD = 1
PIECE = 32
VMEM = 44 * 2**20


def dft_table(frame_len, devices):
    channels = frame_len // 2
    points = np.arange(frame_len)
    turn = np.arange(channels)[:, None] * points[None, :] % frame_len
    wave = np.cos(2 * np.pi * points / frame_len)
    sine = np.sin(2 * np.pi * points / frame_len)
    rows = np.stack([wave[turn], -sine[turn]])
    high = rows.astype(ml_dtypes.bfloat16)
    low = (rows - high.astype(np.float64)).astype(ml_dtypes.bfloat16)
    parts = np.stack([high, low]).reshape(2, 2, devices, 2, QUAD, frame_len)
    return parts.transpose(3, 2, 0, 1, 4, 5).reshape(2, devices // 2, 2, 4 * QUAD, frame_len)


def peer(step):
    inp, tm = lax.axis_index("inp"), lax.axis_index("tm")
    chip = lax.div(step, 2)
    mixed = lax.rem(lax.div(chip, 4) * STRIDE, 16)
    x = lax.rem(lax.div(inp, 2) + lax.div(mixed, 4), 4)
    y = lax.rem(lax.div(tm, 8) * 2 + lax.rem(inp, 2) + mixed, 4)
    z = lax.rem(lax.div(tm, 2) + chip, 4)
    core = lax.rem(tm + step, 2)
    return (x * 2 + lax.rem(y, 2), lax.div(y, 2) * 8 + z * 2 + core), chip * 2 + core


def interleave(value):
    sets = [value[:, :, j * LANES : (j + 1) * LANES] for j in range(QUAD)]
    row = lax.broadcasted_iota(jnp.int32, (1, 8, 1), 1)

    def exchange(first, second, reach):
        keep = lax.rem(lax.div(row, reach), 2) == 0
        low = jnp.where(keep, first, pltpu.roll(second, reach, 1))
        high = jnp.where(keep, pltpu.roll(first, 8 - reach, 1), second)
        return low, high

    near, far = zip(exchange(sets[0], sets[2], 2), exchange(sets[1], sets[3], 2))
    near, far = (near[0], far[0]), (near[1], far[1])
    channels = [*exchange(near[0], far[0], 1), *exchange(near[1], far[1], 1)]
    return jnp.concatenate(channels, axis=1)


def correlate(first, second, scale, vis, at):
    all_inputs = vis.shape[-1]
    sources = first.shape[0]
    inputs = LANES // 2
    inp_count = all_inputs // inputs
    times = sources // inp_count
    lane = lax.broadcasted_iota(jnp.int32, (1, 1, LANES), 2)
    row = lax.broadcasted_iota(jnp.int32, (1, 8, 1), 1)
    sign = jnp.where(row < QUAD, -1.0, 1.0).astype(jnp.float32)
    for c in range(2):
        columns, turned = [], []
        for i in range(0, inp_count, 2):
            low, high = [], []
            for ref in (first, second):
                block = ref[i * times : (i + 2) * times].astype(jnp.float32)
                block = block[:, c * 8 : (c + 1) * 8, :]
                even, odd = block[:times], block[times:]
                low.append(jnp.where(lane < inputs, even, pltpu.roll(odd, inputs, 2)))
                high.append(jnp.where(lane < inputs, pltpu.roll(even, inputs, 2), odd))
            merged = jnp.concatenate(low + high, axis=0)
            swapped = pltpu.roll(merged, QUAD, 1) * sign
            columns.append(merged.reshape(-1, LANES).astype(jnp.bfloat16))
            turned.append(swapped.reshape(-1, LANES).astype(jnp.bfloat16))
        spectra = jnp.concatenate(columns, axis=1)
        quarter = jnp.concatenate(turned, axis=1)
        across = spectra.T
        vis[0, at + c] = jnp.dot(across, spectra, preferred_element_type=jnp.float32) * scale
        vis[1, at + c] = jnp.dot(across, quarter, preferred_element_type=jnp.float32) * scale


def correlate_half(half, early, late, scale, vis, done=None):
    def pair(k, carry):
        rows = pl.ds(pl.multiple_of(k * 16, 16), 16)
        early_rows = pl.ds(pl.multiple_of(half * 8 * QUAD + k * 16, 16), 16)
        correlate(early.at[:, early_rows], late.at[half, :, rows], scale, vis, 2 * k)
        if done is not None:
            done(k)
        return carry

    lax.fori_loop(0, QUAD // 2, pair, 0)


def spectra_kernel(
    total,
    scale,
    samples,
    taps,
    table,
    early,
    late,
    vis,
    raw,
    past_out,
    past_in,
    next_out,
    next_in,
    filtered,
    tab,
    early_box,
    late_box,
    raw_sem,
    tab_sem,
    past_sem,
    next_sem,
    send_sem,
    recv_sem,
    own_sem,
):
    inputs = samples.shape[0]
    tap_count, frame_len = taps.shape
    spec_dev = samples.shape[1] // frame_len
    tm_count = lax.axis_size("tm")
    back = tap_count - 1
    half = spec_dev // 2
    rows = half * inputs
    inp, tm = lax.axis_index("inp"), lax.axis_index("tm")
    me = inp * tm_count + tm
    groups = total // GROUP

    def load(part, first, count):
        cut = pl.ds(first * frame_len, count * frame_len)
        return pltpu.make_async_copy(samples.at[:, cut], raw.at[:, cut], raw_sem.at[part])

    before = back - AHEAD
    quarter = spec_dev // 4
    parts = [(spec_dev - before, before), (0, AHEAD)]
    parts += [(quarter - before, half + back)]
    parts += [(AHEAD, quarter - before - AHEAD), (quarter + half + AHEAD, quarter - AHEAD - before)]

    def fetch(chip):
        place, _ = peer(chip * 2)
        pltpu.make_async_copy(
            table.at[:, lax.div(place[0] * tm_count + place[1], 2)],
            tab.at[:, pl.ds(chip * 2, 2)],
            tab_sem.at[lax.div(chip * 2, GROUP)],
        ).start()

    def fetch_all(first, last):
        def one(chip, carry):
            fetch(chip)
            return carry

        lax.fori_loop(first, last, one, 0)

    for part, (first, count) in enumerate(parts):
        load(part, first, count).start()
    fetch_all(0, GROUP)

    barrier = pltpu.get_barrier_semaphore()

    def greet(step, carry):
        pl.semaphore_signal(barrier, inc=1, device_id=peer(step)[0], device_id_type=MESH)
        return carry

    lax.fori_loop(1, total, greet, 0)

    weights_of = lambda cut: [
        taps[k : k + 1, cut].astype(jnp.float32) for k in range(tap_count)
    ]

    live = jnp.where(tm == tm_count - 1, 0.0, 1.0).astype(jnp.float32)

    def fir(runs):
        def tile(n, carry):
            cut = pl.ds(pl.multiple_of(n * LANES, LANES), LANES)
            weights = weights_of(cut)

            def frame(s):
                if s < 0:
                    at = (s + before) * inputs
                    return past_in[at : at + inputs, cut].astype(jnp.float32)
                if s >= spec_dev:
                    return next_in[:, cut].astype(jnp.float32)
                at = pl.ds(pl.multiple_of(s * frame_len + n * LANES, LANES), LANES)
                return raw[:, at].astype(jnp.float32)

            for first, count, row in runs:
                window = [frame(first - before + k) for k in range(back)]
                for s in range(first, first + count):
                    window.append(frame(s + AHEAD))
                    value = weights[0] * window[0]
                    for k in range(1, back):
                        value = value + weights[k] * window[k]
                    if s + AHEAD == spec_dev:
                        value = value * live
                    value = value + weights[back] * window[back]
                    at = row + (s - first) * inputs
                    filtered[at : at + inputs, cut] = value.astype(jnp.bfloat16)
                    window.pop(0)
            return carry

        lax.fori_loop(0, frame_len // LANES, tile, 0)

    def hand_on(piece):
        cut = pl.ds(piece * PIECE, PIECE)
        return pltpu.make_async_remote_copy(
            past_out.at[cut],
            past_in.at[cut],
            past_sem.at[0],
            past_sem.at[1],
            device_id=(inp, lax.rem(tm + 1, tm_count)),
            device_id_type=MESH,
        )

    def hand_back(piece):
        cut = pl.ds(piece * PIECE, PIECE)
        return pltpu.make_async_remote_copy(
            next_out.at[cut],
            next_in.at[cut],
            next_sem.at[0],
            next_sem.at[1],
            device_id=(inp, lax.rem(tm + tm_count - 1, tm_count)),
            device_id_type=MESH,
        )

    load(0, *parts[0]).wait()
    load(1, *parts[1]).wait()
    for k in range(before):
        first = (spec_dev - before + k) * frame_len
        past_out[k * inputs : (k + 1) * inputs, :] = (
            raw[:, first : first + frame_len].astype(jnp.float32).astype(jnp.bfloat16)
        )
    next_out[...] = raw[:, :frame_len].astype(jnp.float32).astype(jnp.bfloat16)

    pl.semaphore_wait(barrier, total - 1)

    @pl.when(tm < tm_count - 1)
    def _():
        for piece in range(before * inputs // PIECE):
            hand_on(piece).start()

    for piece in range(AHEAD * inputs // PIECE):
        hand_back(piece).start()

    fetch_all(GROUP, total // 2)

    load(2, *parts[2]).wait()
    fir([(quarter, half, rows)])

    def handed_over():
        pltpu.make_async_copy(next_out, next_out, next_sem.at[0]).wait()

        @pl.when(tm < tm_count - 1)
        def _():
            pltpu.make_async_copy(past_out, past_out, past_sem.at[0]).wait()

    boxes = [
        (lambda slot: early_box.at[slot], lambda: early.at[me], early_box, early),
        (lambda slot: late_box.at[0, slot], lambda: late.at[0, me], late_box.at[0], late.at[0]),
        (lambda slot: late_box.at[1, slot], lambda: late.at[1, me], late_box.at[1], late.at[1]),
    ]

    def own(phase):
        source, target = boxes[phase][:2]
        return pltpu.make_async_copy(source(peer(0)[1]), target(), own_sem.at[phase])

    def channelize(phase, base, halves):
        source, target = boxes[phase][:2]

        def group_step(index, carry):
            group = index
            at = pl.ds(group * GROUP, GROUP)
            if phase == 0:

                pltpu.make_async_copy(tab.at[:, at], tab.at[:, at], tab_sem.at[group]).wait()
            frames = filtered[base : base + rows, :]
            for h in halves:
                value = lax.dot_general(
                    tab[h, at].reshape(-1, frame_len),
                    frames,
                    (((1,), (1,)), ((), ())),
                    preferred_element_type=jnp.float32,
                ).reshape(GROUP, 2, 2 * QUAD, -1)
                box = interleave(value[:, 0] + value[:, 1]).astype(jnp.bfloat16)
                if phase == 0:
                    early_box[at, h * 8 * QUAD : (h + 1) * 8 * QUAD] = box
                else:
                    late_box[h, at] = box

            if phase == 0:
                pl.when(index == 0)(handed_over)

            def send(k, carry):
                step = group * GROUP + k
                place, slot = peer(step)

                @pl.when(step == 0)
                def _():
                    own(phase).start()

                @pl.when(step > 0)
                def _():
                    pltpu.make_async_remote_copy(
                        source(slot),
                        target(),
                        send_sem.at[phase],
                        recv_sem.at[phase],
                        device_id=place,
                        device_id_type=MESH,
                    ).start()

                return carry

            lax.fori_loop(0, GROUP, send, 0)
            return carry

        lax.fori_loop(0, groups, group_step, 0)

    channelize(0, rows, (0, 1))

    @pl.when(tm > 0)
    def _():
        pltpu.make_async_copy(past_in, past_in, past_sem.at[1]).wait()

    @pl.when(tm == 0)
    def _():
        past_in[...] = jnp.zeros_like(past_in)

    pltpu.make_async_copy(next_in, next_in, next_sem.at[1]).wait()
    load(3, *parts[3]).wait()
    load(4, *parts[4]).wait()
    fir([(0, quarter, 0), (quarter + half, quarter, quarter * inputs)])
    channelize(1, 0, (0,))
    channelize(2, 0, (1,))

    others = pl.ds(0, total - 1)

    def arrive(phase):
        came = boxes[phase][3].at[others]
        own(phase).wait()
        pltpu.make_async_copy(came, came, recv_sem.at[phase]).wait()

    arrive(0)
    arrive(1)
    correlate_half(0, early, late, scale, vis)
    arrive(2)
    for phase in range(3):
        sent = boxes[phase][2].at[others]
        pltpu.make_async_copy(sent, sent, send_sem.at[phase]).wait()


def correlate_kernel(scale, early, late, vis, out, rest, sem):
    def write(source, k, first):
        pair = pl.ds(2 * k, 2)
        return pltpu.make_async_copy(source.at[:, pair], out.at[:, pl.ds(first + 2 * k, 2)], sem)

    def begin(k, carry):
        write(vis, k, 0).start()
        return carry

    lax.fori_loop(0, QUAD // 2, begin, 0)
    correlate_half(1, early, late, scale, rest, lambda k: write(rest, k, QUAD).start())
    pltpu.make_async_copy(out, out, sem).wait()


def on_device(table, samples, filter_taps):
    inputs = samples.shape[0]
    tap_count, frame_len = filter_taps.shape
    spec_dev = samples.shape[1] // frame_len
    inp_count, tm_count = lax.axis_size("inp"), lax.axis_size("tm")
    total = inp_count * tm_count
    chan_dev = frame_len // 2 // total
    groups = total // GROUP
    all_inputs = inputs * inp_count
    bf16 = jnp.bfloat16
    scale = 1.0 / (16384.0**2 * frame_len * spec_dev * tm_count)
    early_shape = (total, 16 * QUAD, LANES)
    late_shape = (2, total, 8 * QUAD, LANES)
    vis_shape = (2, QUAD, all_inputs, all_inputs)
    hbm = pl.BlockSpec(memory_space=pltpu.HBM)
    vmem = pl.BlockSpec(memory_space=pltpu.VMEM)
    early, late, vis = pl.pallas_call(
        functools.partial(spectra_kernel, total, scale),
        out_shape=[
            pltpu.VMEM(early_shape, bf16),
            pltpu.VMEM(late_shape, bf16),
            pltpu.VMEM(vis_shape, jnp.float32),
        ],
        in_specs=[hbm, vmem, hbm],
        out_specs=[vmem, vmem, vmem],
        scratch_shapes=[
            pltpu.VMEM(samples.shape, jnp.int32),
            pltpu.VMEM(((tap_count - 1 - AHEAD) * inputs, frame_len), bf16),
            pltpu.VMEM(((tap_count - 1 - AHEAD) * inputs, frame_len), bf16),
            pltpu.VMEM((AHEAD * inputs, frame_len), bf16),
            pltpu.VMEM((AHEAD * inputs, frame_len), bf16),
            pltpu.VMEM((spec_dev * inputs, frame_len), bf16),
            pltpu.VMEM((2, total, 4 * QUAD, frame_len), bf16),
            pltpu.VMEM(early_shape, bf16),
            pltpu.VMEM(late_shape, bf16),
            pltpu.SemaphoreType.DMA((5,)),
            pltpu.SemaphoreType.DMA((groups,)),
            pltpu.SemaphoreType.DMA((2,)),
            pltpu.SemaphoreType.DMA((2,)),
            pltpu.SemaphoreType.DMA((3,)),
            pltpu.SemaphoreType.DMA((3,)),
            pltpu.SemaphoreType.DMA((3,)),
        ],
        compiler_params=pltpu.CompilerParams(
            collective_id=0, has_side_effects=True, vmem_limit_bytes=VMEM
        ),
        name="channelize_and_exchange",
    )(samples, filter_taps, table)
    return pl.pallas_call(
        functools.partial(correlate_kernel, scale),
        out_shape=jax.ShapeDtypeStruct((2, chan_dev, all_inputs, all_inputs), jnp.float32),
        in_specs=[vmem, vmem, vmem],
        out_specs=hbm,
        scratch_shapes=[pltpu.VMEM(vis_shape, jnp.float32), pltpu.SemaphoreType.DMA],
        compiler_params=pltpu.CompilerParams(vmem_limit_bytes=VMEM // 2),
        name="correlate",
    )(early, late, vis)


def solution(mesh):
    devices = mesh.size
    table = dft_table(2048, devices)

    def whole(samples, filter_taps):
        return jax.shard_map(
            on_device,
            mesh=mesh,
            in_specs=(P(), P("inp", "tm"), P()),
            out_specs=P(None, ("inp", "tm"), None, None),
            check_vma=False,
        )(jnp.asarray(table), samples, filter_taps)

    return whole
```

```python
import functools

import jax
import jax.numpy as jnp
import ml_dtypes
import numpy as np
from jax import lax
from jax.experimental import pallas as pl
from jax.experimental.pallas import tpu as pltpu
from jax.sharding import PartitionSpec as P

MESH = pl.DeviceIdType.MESH
LANES = 128
QUAD = 4
GROUP = 16
STRIDE = 11
AHEAD = 1
PIECE = 32
VMEM = 44 * 2**20


def dft_table(frame_len, devices):
    channels = frame_len // 2
    points = np.arange(frame_len)
    turn = np.arange(channels)[:, None] * points[None, :] % frame_len
    wave = np.cos(2 * np.pi * points / frame_len)
    sine = np.sin(2 * np.pi * points / frame_len)
    rows = np.stack([wave[turn], -sine[turn]])
    high = rows.astype(ml_dtypes.bfloat16)
    low = (rows - high.astype(np.float64)).astype(ml_dtypes.bfloat16)
    parts = np.stack([high, low]).reshape(2, 2, devices, 2, QUAD, frame_len)
    return parts.transpose(3, 2, 0, 1, 4, 5).reshape(2, devices // 2, 2, 4 * QUAD, frame_len)


def peer(group, step):
    inp, tm = lax.axis_index("inp"), lax.axis_index("tm")
    chip = group * (GROUP // 2) + lax.div(step, 2)
    mixed = lax.rem((group * (GROUP // 8) + lax.div(step, 8)) * STRIDE, 16)
    x = lax.rem(lax.div(inp, 2) + lax.div(mixed, 4), 4)
    y = lax.rem(lax.div(tm, 8) * 2 + lax.rem(inp, 2) + mixed, 4)
    z = lax.rem(lax.div(tm, 2) + lax.div(step, 2), 4)
    core = lax.rem(tm + step, 2)
    return (x * 2 + lax.rem(y, 2), lax.div(y, 2) * 8 + z * 2 + core), chip * 2 + core


def interleave(value):
    sets = [value[:, :, j * LANES : (j + 1) * LANES] for j in range(QUAD)]
    row = lax.broadcasted_iota(jnp.int32, (1, 8, 1), 1)

    def exchange(first, second, reach):
        keep = lax.rem(lax.div(row, reach), 2) == 0
        low = jnp.where(keep, first, pltpu.roll(second, reach, 1))
        high = jnp.where(keep, pltpu.roll(first, 8 - reach, 1), second)
        return low, high

    near, far = zip(exchange(sets[0], sets[2], 2), exchange(sets[1], sets[3], 2))
    near, far = (near[0], far[0]), (near[1], far[1])
    channels = [*exchange(near[0], far[0], 1), *exchange(near[1], far[1], 1)]
    return jnp.concatenate(channels, axis=1)


def correlate(first, second, scale, vis, at):
    all_inputs = vis.shape[-1]
    sources = first.shape[0]
    inputs = LANES // 2
    inp_count = all_inputs // inputs
    times = sources // inp_count
    lane = lax.broadcasted_iota(jnp.int32, (1, 1, LANES), 2)
    row = lax.broadcasted_iota(jnp.int32, (1, 8, 1), 1)
    sign = jnp.where(row < QUAD, -1.0, 1.0).astype(jnp.float32)
    for c in range(2):
        columns, turned = [], []
        for i in range(0, inp_count, 2):
            low, high = [], []
            for ref in (first, second):
                block = ref[i * times : (i + 2) * times].astype(jnp.float32)
                block = block[:, c * 8 : (c + 1) * 8, :]
                even, odd = block[:times], block[times:]
                low.append(jnp.where(lane < inputs, even, pltpu.roll(odd, inputs, 2)))
                high.append(jnp.where(lane < inputs, pltpu.roll(even, inputs, 2), odd))
            merged = jnp.concatenate(low + high, axis=0)
            swapped = pltpu.roll(merged, QUAD, 1) * sign
            columns.append(merged.reshape(-1, LANES).astype(jnp.bfloat16))
            turned.append(swapped.reshape(-1, LANES).astype(jnp.bfloat16))
        spectra = jnp.concatenate(columns, axis=1)
        quarter = jnp.concatenate(turned, axis=1)
        across = spectra.T
        vis[0, at + c] = jnp.dot(across, spectra, preferred_element_type=jnp.float32) * scale
        vis[1, at + c] = jnp.dot(across, quarter, preferred_element_type=jnp.float32) * scale


def correlate_half(half, early, late, scale, vis, done=None):
    def pair(k, carry):
        rows = pl.ds(pl.multiple_of(k * 16, 16), 16)
        early_rows = pl.ds(pl.multiple_of(half * 8 * QUAD + k * 16, 16), 16)
        correlate(early.at[:, early_rows], late.at[half, :, rows], scale, vis, 2 * k)
        if done is not None:
            done(k)
        return carry

    lax.fori_loop(0, QUAD // 2, pair, 0)


def spectra_kernel(
    total,
    scale,
    samples,
    taps,
    table,
    early,
    late,
    vis,
    raw,
    past_out,
    past_in,
    next_out,
    next_in,
    filtered,
    tab,
    early_box,
    late_box,
    raw_sem,
    tab_sem,
    past_sem,
    next_sem,
    send_sem,
    recv_sem,
    own_sem,
):
    inputs = samples.shape[0]
    tap_count, frame_len = taps.shape
    spec_dev = samples.shape[1] // frame_len
    tm_count = lax.axis_size("tm")
    back = tap_count - 1
    half = spec_dev // 2
    rows = half * inputs
    inp, tm = lax.axis_index("inp"), lax.axis_index("tm")
    me = inp * tm_count + tm
    groups = total // GROUP

    def load(part, first, count):
        cut = pl.ds(first * frame_len, count * frame_len)
        return pltpu.make_async_copy(samples.at[:, cut], raw.at[:, cut], raw_sem.at[part])

    before = back - AHEAD
    quarter = spec_dev // 4
    parts = [(spec_dev - before, before), (0, AHEAD)]
    parts += [(quarter - before, half + back)]
    parts += [(AHEAD, quarter - before - AHEAD), (quarter + half + AHEAD, quarter - AHEAD - before)]

    def fetch(chip):
        place, _ = peer(0, chip * 2)
        pltpu.make_async_copy(
            table.at[:, lax.div(place[0] * tm_count + place[1], 2)],
            tab.at[:, pl.ds(chip * 2, 2)],
            tab_sem.at[lax.div(chip * 2, GROUP)],
        ).start()

    def fetch_all(first, last):
        def one(chip, carry):
            fetch(chip)
            return carry

        lax.fori_loop(first, last, one, 0)

    def load_all(first, last):
        for part in range(first, last):
            load(part, *parts[part]).start()

    load_all(0, 2)
    barrier = pltpu.get_barrier_semaphore()

    def greet(group, first):
        for k in range(first, GROUP):
            pl.semaphore_signal(barrier, inc=1, device_id=peer(group, k)[0], device_id_type=MESH)
        return 0

    for group in range(groups):
        greet(group, 1 if group == 0 else 0)

    weights_of = lambda cut: [
        taps[k : k + 1, cut].astype(jnp.float32) for k in range(tap_count)
    ]

    live = jnp.where(tm == tm_count - 1, 0.0, 1.0).astype(jnp.float32)

    def fir(runs):
        def tile(n, carry):
            cut = pl.ds(pl.multiple_of(n * LANES, LANES), LANES)
            weights = weights_of(cut)

            def frame(s):
                if s < 0:
                    at = (s + before) * inputs
                    return past_in[at : at + inputs, cut].astype(jnp.float32)
                if s >= spec_dev:
                    return next_in[:, cut].astype(jnp.float32)
                at = pl.ds(pl.multiple_of(s * frame_len + n * LANES, LANES), LANES)
                return raw[:, at].astype(jnp.float32)

            for first, count, row in runs:
                window = [frame(first - before + k) for k in range(back)]
                for s in range(first, first + count):
                    window.append(frame(s + AHEAD))
                    value = weights[0] * window[0]
                    for k in range(1, back):
                        value = value + weights[k] * window[k]
                    if s + AHEAD == spec_dev:
                        value = value * live
                    value = value + weights[back] * window[back]
                    at = row + (s - first) * inputs
                    filtered[at : at + inputs, cut] = value.astype(jnp.bfloat16)
                    window.pop(0)
            return carry

        lax.fori_loop(0, frame_len // LANES, tile, 0)

    def hand_on(piece):
        cut = pl.ds(piece * PIECE, PIECE)
        return pltpu.make_async_remote_copy(
            past_out.at[cut],
            past_in.at[cut],
            past_sem.at[0],
            past_sem.at[1],
            device_id=(inp, lax.rem(tm + 1, tm_count)),
            device_id_type=MESH,
        )

    def hand_back(piece):
        cut = pl.ds(piece * PIECE, PIECE)
        return pltpu.make_async_remote_copy(
            next_out.at[cut],
            next_in.at[cut],
            next_sem.at[0],
            next_sem.at[1],
            device_id=(inp, lax.rem(tm + tm_count - 1, tm_count)),
            device_id_type=MESH,
        )

    load_all(2, 3)
    fetch_all(0, GROUP // 2)
    load_all(3, 5)
    load(0, *parts[0]).wait()
    load(1, *parts[1]).wait()
    for k in range(before):
        first = (spec_dev - before + k) * frame_len
        past_out[k * inputs : (k + 1) * inputs, :] = (
            raw[:, first : first + frame_len].astype(jnp.float32).astype(jnp.bfloat16)
        )
    next_out[...] = raw[:, :frame_len].astype(jnp.float32).astype(jnp.bfloat16)

    pl.semaphore_wait(barrier, total - 1)

    @pl.when(tm < tm_count - 1)
    def _():
        for piece in range(before * inputs // PIECE):
            hand_on(piece).start()

    for piece in range(AHEAD * inputs // PIECE):
        hand_back(piece).start()

    fetch_all(GROUP // 2, total // 2)

    load(2, *parts[2]).wait()
    fir([(quarter, half, rows)])

    def handed_over():
        pltpu.make_async_copy(next_out, next_out, next_sem.at[0]).wait()

        @pl.when(tm < tm_count - 1)
        def _():
            pltpu.make_async_copy(past_out, past_out, past_sem.at[0]).wait()

    boxes = [
        (lambda slot: early_box.at[slot], lambda: early.at[me], early_box, early),
        (lambda slot: late_box.at[0, slot], lambda: late.at[0, me], late_box.at[0], late.at[0]),
        (lambda slot: late_box.at[1, slot], lambda: late.at[1, me], late_box.at[1], late.at[1]),
    ]

    def own(phase):
        source, target = boxes[phase][:2]
        return pltpu.make_async_copy(source(peer(0, 0)[1]), target(), own_sem.at[phase])

    def channelize(phase, base, halves):
        source, target = boxes[phase][:2]

        def group_step(index, carry):
            group = index
            at = pl.ds(group * GROUP, GROUP)
            if phase == 0:

                pltpu.make_async_copy(tab.at[:, at], tab.at[:, at], tab_sem.at[group]).wait()
            frames = filtered[base : base + rows, :]
            for h in halves:
                value = lax.dot_general(
                    tab[h, at].reshape(-1, frame_len),
                    frames,
                    (((1,), (1,)), ((), ())),
                    preferred_element_type=jnp.float32,
                ).reshape(GROUP, 2, 2 * QUAD, -1)
                box = interleave(value[:, 0] + value[:, 1]).astype(jnp.bfloat16)
                if phase == 0:
                    early_box[at, h * 8 * QUAD : (h + 1) * 8 * QUAD] = box
                else:
                    late_box[h, at] = box

            if phase == 0:
                pl.when(index == 0)(handed_over)

            def send(place, slot):
                pltpu.make_async_remote_copy(
                    source(slot),
                    target(),
                    send_sem.at[phase],
                    recv_sem.at[phase],
                    device_id=place,
                    device_id_type=MESH,
                ).start()

            @pl.when(index == 0)
            def _():
                own(phase).start()

            @pl.when(index > 0)
            def _():
                send(*peer(group, 0))

            for k in range(1, GROUP):
                send(*peer(group, k))
            return carry

        lax.fori_loop(0, groups, group_step, 0)

    channelize(0, rows, (0, 1))

    @pl.when(tm > 0)
    def _():
        pltpu.make_async_copy(past_in, past_in, past_sem.at[1]).wait()

    @pl.when(tm == 0)
    def _():
        past_in[...] = jnp.zeros_like(past_in)

    pltpu.make_async_copy(next_in, next_in, next_sem.at[1]).wait()
    load(3, *parts[3]).wait()
    load(4, *parts[4]).wait()
    fir([(0, quarter, 0), (quarter + half, quarter, quarter * inputs)])
    channelize(1, 0, (0,))
    channelize(2, 0, (1,))

    others = pl.ds(0, total - 1)

    def arrive(phase):
        came = boxes[phase][3].at[others]
        own(phase).wait()
        pltpu.make_async_copy(came, came, recv_sem.at[phase]).wait()

    arrive(0)
    arrive(1)
    correlate_half(0, early, late, scale, vis)
    arrive(2)
    for phase in range(3):
        sent = boxes[phase][2].at[others]
        pltpu.make_async_copy(sent, sent, send_sem.at[phase]).wait()


def correlate_kernel(scale, early, late, vis, out, rest, sem):
    def write(source, k, first):
        pair = pl.ds(2 * k, 2)
        return pltpu.make_async_copy(source.at[:, pair], out.at[:, pl.ds(first + 2 * k, 2)], sem)

    def begin(k, carry):
        write(vis, k, 0).start()
        return carry

    lax.fori_loop(0, QUAD // 2, begin, 0)
    correlate_half(1, early, late, scale, rest, lambda k: write(rest, k, QUAD).start())
    pltpu.make_async_copy(out, out, sem).wait()


def on_device(table, samples, filter_taps):
    inputs = samples.shape[0]
    tap_count, frame_len = filter_taps.shape
    spec_dev = samples.shape[1] // frame_len
    inp_count, tm_count = lax.axis_size("inp"), lax.axis_size("tm")
    total = inp_count * tm_count
    chan_dev = frame_len // 2 // total
    groups = total // GROUP
    all_inputs = inputs * inp_count
    bf16 = jnp.bfloat16
    scale = 1.0 / (16384.0**2 * frame_len * spec_dev * tm_count)
    early_shape = (total, 16 * QUAD, LANES)
    late_shape = (2, total, 8 * QUAD, LANES)
    vis_shape = (2, QUAD, all_inputs, all_inputs)
    hbm = pl.BlockSpec(memory_space=pltpu.HBM)
    vmem = pl.BlockSpec(memory_space=pltpu.VMEM)
    early, late, vis = pl.pallas_call(
        functools.partial(spectra_kernel, total, scale),
        out_shape=[
            pltpu.VMEM(early_shape, bf16),
            pltpu.VMEM(late_shape, bf16),
            pltpu.VMEM(vis_shape, jnp.float32),
        ],
        in_specs=[hbm, vmem, hbm],
        out_specs=[vmem, vmem, vmem],
        scratch_shapes=[
            pltpu.VMEM(samples.shape, jnp.int32),
            pltpu.VMEM(((tap_count - 1 - AHEAD) * inputs, frame_len), bf16),
            pltpu.VMEM(((tap_count - 1 - AHEAD) * inputs, frame_len), bf16),
            pltpu.VMEM((AHEAD * inputs, frame_len), bf16),
            pltpu.VMEM((AHEAD * inputs, frame_len), bf16),
            pltpu.VMEM((spec_dev * inputs, frame_len), bf16),
            pltpu.VMEM((2, total, 4 * QUAD, frame_len), bf16),
            pltpu.VMEM(early_shape, bf16),
            pltpu.VMEM(late_shape, bf16),
            pltpu.SemaphoreType.DMA((5,)),
            pltpu.SemaphoreType.DMA((groups,)),
            pltpu.SemaphoreType.DMA((2,)),
            pltpu.SemaphoreType.DMA((2,)),
            pltpu.SemaphoreType.DMA((3,)),
            pltpu.SemaphoreType.DMA((3,)),
            pltpu.SemaphoreType.DMA((3,)),
        ],
        compiler_params=pltpu.CompilerParams(
            collective_id=0, has_side_effects=True, vmem_limit_bytes=VMEM
        ),
        name="channelize_and_exchange",
    )(samples, filter_taps, table)
    return pl.pallas_call(
        functools.partial(correlate_kernel, scale),
        out_shape=jax.ShapeDtypeStruct((2, chan_dev, all_inputs, all_inputs), jnp.float32),
        in_specs=[vmem, vmem, vmem],
        out_specs=hbm,
        scratch_shapes=[pltpu.VMEM(vis_shape, jnp.float32), pltpu.SemaphoreType.DMA],
        compiler_params=pltpu.CompilerParams(vmem_limit_bytes=VMEM // 2),
        name="correlate",
    )(early, late, vis)


def solution(mesh):
    devices = mesh.size
    table = dft_table(2048, devices)

    def whole(samples, filter_taps):
        return jax.shard_map(
            on_device,
            mesh=mesh,
            in_specs=(P(), P("inp", "tm"), P()),
            out_specs=P(None, ("inp", "tm"), None, None),
            check_vma=False,
        )(jnp.asarray(table), samples, filter_taps)

    return whole
```

```python
import functools

import jax
import jax.numpy as jnp
import ml_dtypes
import numpy as np
from jax import lax
from jax.experimental import pallas as pl
from jax.experimental.pallas import tpu as pltpu
from jax.sharding import PartitionSpec as P

MESH = pl.DeviceIdType.MESH
LANES = 128
QUAD = 4
GROUP = 16
STRIDE = 9
AHEAD = 1
PIECE = 32
VMEM = 44 * 2**20


def dft_table(frame_len, devices):
    channels = frame_len // 2
    points = np.arange(frame_len)
    turn = np.arange(channels)[:, None] * points[None, :] % frame_len
    wave = np.cos(2 * np.pi * points / frame_len)
    sine = np.sin(2 * np.pi * points / frame_len)
    rows = np.stack([wave[turn], -sine[turn]])
    high = rows.astype(ml_dtypes.bfloat16)
    low = (rows - high.astype(np.float64)).astype(ml_dtypes.bfloat16)
    parts = np.stack([high, low]).reshape(2, 2, devices, 2, QUAD, frame_len)
    return parts.transpose(3, 2, 0, 1, 4, 5).reshape(2, devices // 2, 2, 4 * QUAD, frame_len)


def peer(group, step):
    inp, tm = lax.axis_index("inp"), lax.axis_index("tm")
    chip = group * (GROUP // 2) + lax.div(step, 2)
    mixed = lax.rem((group * (GROUP // 8) + lax.div(step, 8)) * STRIDE, 16)
    x = lax.rem(lax.div(inp, 2) + lax.div(mixed, 4), 4)
    y = lax.rem(lax.div(tm, 8) * 2 + lax.rem(inp, 2) + mixed, 4)
    z = lax.rem(lax.div(tm, 2) + lax.div(step, 2), 4)
    core = lax.rem(tm + step, 2)
    return (x * 2 + lax.rem(y, 2), lax.div(y, 2) * 8 + z * 2 + core), chip * 2 + core


def interleave(value):
    sets = [value[:, :, j * LANES : (j + 1) * LANES] for j in range(QUAD)]
    row = lax.broadcasted_iota(jnp.int32, (1, 8, 1), 1)

    def exchange(first, second, reach):
        keep = lax.rem(lax.div(row, reach), 2) == 0
        low = jnp.where(keep, first, pltpu.roll(second, reach, 1))
        high = jnp.where(keep, pltpu.roll(first, 8 - reach, 1), second)
        return low, high

    near, far = zip(exchange(sets[0], sets[2], 2), exchange(sets[1], sets[3], 2))
    near, far = (near[0], far[0]), (near[1], far[1])
    channels = [*exchange(near[0], far[0], 1), *exchange(near[1], far[1], 1)]
    return jnp.concatenate(channels, axis=1)


def correlate(first, second, scale, vis, at):
    all_inputs = vis.shape[-1]
    sources = first.shape[0]
    inputs = LANES // 2
    inp_count = all_inputs // inputs
    times = sources // inp_count
    lane = lax.broadcasted_iota(jnp.int32, (1, 1, LANES), 2)
    row = lax.broadcasted_iota(jnp.int32, (1, 8, 1), 1)
    sign = jnp.where(row < QUAD, -1.0, 1.0).astype(jnp.float32)
    for c in range(2):
        columns, turned = [], []
        for i in range(0, inp_count, 2):
            low, high = [], []
            for ref in (first, second):
                block = ref[i * times : (i + 2) * times].astype(jnp.float32)
                block = block[:, c * 8 : (c + 1) * 8, :]
                even, odd = block[:times], block[times:]
                low.append(jnp.where(lane < inputs, even, pltpu.roll(odd, inputs, 2)))
                high.append(jnp.where(lane < inputs, pltpu.roll(even, inputs, 2), odd))
            merged = jnp.concatenate(low + high, axis=0)
            swapped = pltpu.roll(merged, QUAD, 1) * sign
            columns.append(merged.reshape(-1, LANES).astype(jnp.bfloat16))
            turned.append(swapped.reshape(-1, LANES).astype(jnp.bfloat16))
        spectra = jnp.concatenate(columns, axis=1)
        quarter = jnp.concatenate(turned, axis=1)
        across = spectra.T
        vis[0, at + c] = jnp.dot(across, spectra, preferred_element_type=jnp.float32) * scale
        vis[1, at + c] = jnp.dot(across, quarter, preferred_element_type=jnp.float32) * scale


def correlate_half(half, early, late, scale, vis, done=None):
    def pair(k, carry):
        rows = pl.ds(pl.multiple_of(k * 16, 16), 16)
        early_rows = pl.ds(pl.multiple_of(half * 8 * QUAD + k * 16, 16), 16)
        correlate(early.at[:, early_rows], late.at[half, :, rows], scale, vis, 2 * k)
        if done is not None:
            done(k)
        return carry

    lax.fori_loop(0, QUAD // 2, pair, 0)


def spectra_kernel(
    total,
    scale,
    samples,
    taps,
    table,
    early,
    late,
    vis,
    raw,
    past_out,
    past_in,
    next_out,
    next_in,
    filtered,
    tab,
    early_box,
    late_box,
    raw_sem,
    tab_sem,
    past_sem,
    next_sem,
    send_sem,
    recv_sem,
    own_sem,
):
    inputs = samples.shape[0]
    tap_count, frame_len = taps.shape
    spec_dev = samples.shape[1] // frame_len
    tm_count = lax.axis_size("tm")
    back = tap_count - 1
    half = spec_dev // 2
    rows = half * inputs
    inp, tm = lax.axis_index("inp"), lax.axis_index("tm")
    me = inp * tm_count + tm
    groups = total // GROUP

    def load(part, first, count):
        cut = pl.ds(first * frame_len, count * frame_len)
        return pltpu.make_async_copy(samples.at[:, cut], raw.at[:, cut], raw_sem.at[part])

    before = back - AHEAD
    quarter = spec_dev // 4
    parts = [(spec_dev - before, before), (0, AHEAD)]
    parts += [(quarter - before, half + back)]
    parts += [(AHEAD, quarter - before - AHEAD), (quarter + half + AHEAD, quarter - AHEAD - before)]

    def fetch(chip):
        place, _ = peer(0, chip * 2)
        pltpu.make_async_copy(
            table.at[:, lax.div(place[0] * tm_count + place[1], 2)],
            tab.at[:, pl.ds(chip * 2, 2)],
            tab_sem.at[lax.div(chip * 2, GROUP)],
        ).start()

    def fetch_all(first, last):
        def one(chip, carry):
            fetch(chip)
            return carry

        lax.fori_loop(first, last, one, 0)

    def load_all(first, last):
        for part in range(first, last):
            load(part, *parts[part]).start()

    load_all(0, 2)
    barrier = pltpu.get_barrier_semaphore()

    def greet(group, first):
        for k in range(first, GROUP):
            pl.semaphore_signal(barrier, inc=1, device_id=peer(group, k)[0], device_id_type=MESH)
        return 0

    for group in range(groups):
        greet(group, 1 if group == 0 else 0)

    weights_of = lambda cut: [
        taps[k : k + 1, cut].astype(jnp.float32) for k in range(tap_count)
    ]

    live = jnp.where(tm == tm_count - 1, 0.0, 1.0).astype(jnp.float32)

    def fir(runs):
        def tile(n, carry):
            cut = pl.ds(pl.multiple_of(n * LANES, LANES), LANES)
            weights = weights_of(cut)

            def frame(s):
                if s < 0:
                    at = (s + before) * inputs
                    return past_in[at : at + inputs, cut].astype(jnp.float32)
                if s >= spec_dev:
                    return next_in[:, cut].astype(jnp.float32)
                at = pl.ds(pl.multiple_of(s * frame_len + n * LANES, LANES), LANES)
                return raw[:, at].astype(jnp.float32)

            for first, count, row in runs:
                window = [frame(first - before + k) for k in range(back)]
                for s in range(first, first + count):
                    window.append(frame(s + AHEAD))
                    value = weights[0] * window[0]
                    for k in range(1, back):
                        value = value + weights[k] * window[k]
                    if s + AHEAD == spec_dev:
                        value = value * live
                    value = value + weights[back] * window[back]
                    at = row + (s - first) * inputs
                    filtered[at : at + inputs, cut] = value.astype(jnp.bfloat16)
                    window.pop(0)
            return carry

        lax.fori_loop(0, frame_len // LANES, tile, 0)

    def hand_on(piece):
        cut = pl.ds(piece * PIECE, PIECE)
        return pltpu.make_async_remote_copy(
            past_out.at[cut],
            past_in.at[cut],
            past_sem.at[0],
            past_sem.at[1],
            device_id=(inp, lax.rem(tm + 1, tm_count)),
            device_id_type=MESH,
        )

    def hand_back(piece):
        cut = pl.ds(piece * PIECE, PIECE)
        return pltpu.make_async_remote_copy(
            next_out.at[cut],
            next_in.at[cut],
            next_sem.at[0],
            next_sem.at[1],
            device_id=(inp, lax.rem(tm + tm_count - 1, tm_count)),
            device_id_type=MESH,
        )

    load_all(2, 3)
    fetch_all(0, GROUP // 2)
    load_all(3, 5)
    load(0, *parts[0]).wait()
    load(1, *parts[1]).wait()
    for k in range(before):
        first = (spec_dev - before + k) * frame_len
        past_out[k * inputs : (k + 1) * inputs, :] = (
            raw[:, first : first + frame_len].astype(jnp.float32).astype(jnp.bfloat16)
        )
    next_out[...] = raw[:, :frame_len].astype(jnp.float32).astype(jnp.bfloat16)

    pl.semaphore_wait(barrier, total - 1)

    @pl.when(tm < tm_count - 1)
    def _():
        for piece in range(before * inputs // PIECE):
            hand_on(piece).start()

    for piece in range(AHEAD * inputs // PIECE):
        hand_back(piece).start()

    fetch_all(GROUP // 2, total // 2)

    load(2, *parts[2]).wait()
    fir([(quarter, half, rows)])

    def handed_over():
        pltpu.make_async_copy(next_out, next_out, next_sem.at[0]).wait()

        @pl.when(tm < tm_count - 1)
        def _():
            pltpu.make_async_copy(past_out, past_out, past_sem.at[0]).wait()

    boxes = [
        (lambda slot: early_box.at[slot], lambda: early.at[me], early_box, early),
        (lambda slot: late_box.at[0, slot], lambda: late.at[0, me], late_box.at[0], late.at[0]),
        (lambda slot: late_box.at[1, slot], lambda: late.at[1, me], late_box.at[1], late.at[1]),
    ]

    def own(phase):
        source, target = boxes[phase][:2]
        return pltpu.make_async_copy(source(peer(0, 0)[1]), target(), own_sem.at[phase])

    def channelize(phase, base, halves):
        source, target = boxes[phase][:2]

        def group_step(index, carry):
            group = index
            at = pl.ds(group * GROUP, GROUP)
            if phase == 0:

                pltpu.make_async_copy(tab.at[:, at], tab.at[:, at], tab_sem.at[group]).wait()
            frames = filtered[base : base + rows, :]
            for h in halves:
                value = lax.dot_general(
                    tab[h, at].reshape(-1, frame_len),
                    frames,
                    (((1,), (1,)), ((), ())),
                    preferred_element_type=jnp.float32,
                ).reshape(GROUP, 2, 2 * QUAD, -1)
                box = interleave(value[:, 0] + value[:, 1]).astype(jnp.bfloat16)
                if phase == 0:
                    early_box[at, h * 8 * QUAD : (h + 1) * 8 * QUAD] = box
                else:
                    late_box[h, at] = box

            if phase == 0:
                pl.when(index == 0)(handed_over)

            def send(place, slot):
                pltpu.make_async_remote_copy(
                    source(slot),
                    target(),
                    send_sem.at[phase],
                    recv_sem.at[phase],
                    device_id=place,
                    device_id_type=MESH,
                ).start()

            @pl.when(index == 0)
            def _():
                own(phase).start()

            @pl.when(index > 0)
            def _():
                send(*peer(group, 0))

            for k in range(1, GROUP):
                send(*peer(group, k))
            return carry

        lax.fori_loop(0, groups, group_step, 0)

    channelize(0, rows, (0, 1))

    @pl.when(tm > 0)
    def _():
        pltpu.make_async_copy(past_in, past_in, past_sem.at[1]).wait()

    @pl.when(tm == 0)
    def _():
        past_in[...] = jnp.zeros_like(past_in)

    pltpu.make_async_copy(next_in, next_in, next_sem.at[1]).wait()
    load(3, *parts[3]).wait()
    load(4, *parts[4]).wait()
    fir([(0, quarter, 0), (quarter + half, quarter, quarter * inputs)])
    channelize(1, 0, (0,))
    channelize(2, 0, (1,))

    others = pl.ds(0, total - 1)

    def arrive(phase):
        came = boxes[phase][3].at[others]
        own(phase).wait()
        pltpu.make_async_copy(came, came, recv_sem.at[phase]).wait()

    arrive(0)
    arrive(1)
    correlate_half(0, early, late, scale, vis)
    arrive(2)
    for phase in range(3):
        sent = boxes[phase][2].at[others]
        pltpu.make_async_copy(sent, sent, send_sem.at[phase]).wait()


def correlate_kernel(scale, early, late, vis, out, rest, sem):
    def write(source, k, first):
        pair = pl.ds(2 * k, 2)
        return pltpu.make_async_copy(source.at[:, pair], out.at[:, pl.ds(first + 2 * k, 2)], sem)

    def begin(k, carry):
        write(vis, k, 0).start()
        return carry

    lax.fori_loop(0, QUAD // 2, begin, 0)
    correlate_half(1, early, late, scale, rest, lambda k: write(rest, k, QUAD).start())
    pltpu.make_async_copy(out, out, sem).wait()


def on_device(table, samples, filter_taps):
    inputs = samples.shape[0]
    tap_count, frame_len = filter_taps.shape
    spec_dev = samples.shape[1] // frame_len
    inp_count, tm_count = lax.axis_size("inp"), lax.axis_size("tm")
    total = inp_count * tm_count
    chan_dev = frame_len // 2 // total
    groups = total // GROUP
    all_inputs = inputs * inp_count
    bf16 = jnp.bfloat16
    scale = 1.0 / (16384.0**2 * frame_len * spec_dev * tm_count)
    early_shape = (total, 16 * QUAD, LANES)
    late_shape = (2, total, 8 * QUAD, LANES)
    vis_shape = (2, QUAD, all_inputs, all_inputs)
    hbm = pl.BlockSpec(memory_space=pltpu.HBM)
    vmem = pl.BlockSpec(memory_space=pltpu.VMEM)
    early, late, vis = pl.pallas_call(
        functools.partial(spectra_kernel, total, scale),
        out_shape=[
            pltpu.VMEM(early_shape, bf16),
            pltpu.VMEM(late_shape, bf16),
            pltpu.VMEM(vis_shape, jnp.float32),
        ],
        in_specs=[hbm, vmem, hbm],
        out_specs=[vmem, vmem, vmem],
        scratch_shapes=[
            pltpu.VMEM(samples.shape, jnp.int32),
            pltpu.VMEM(((tap_count - 1 - AHEAD) * inputs, frame_len), bf16),
            pltpu.VMEM(((tap_count - 1 - AHEAD) * inputs, frame_len), bf16),
            pltpu.VMEM((AHEAD * inputs, frame_len), bf16),
            pltpu.VMEM((AHEAD * inputs, frame_len), bf16),
            pltpu.VMEM((spec_dev * inputs, frame_len), bf16),
            pltpu.VMEM((2, total, 4 * QUAD, frame_len), bf16),
            pltpu.VMEM(early_shape, bf16),
            pltpu.VMEM(late_shape, bf16),
            pltpu.SemaphoreType.DMA((5,)),
            pltpu.SemaphoreType.DMA((groups,)),
            pltpu.SemaphoreType.DMA((2,)),
            pltpu.SemaphoreType.DMA((2,)),
            pltpu.SemaphoreType.DMA((3,)),
            pltpu.SemaphoreType.DMA((3,)),
            pltpu.SemaphoreType.DMA((3,)),
        ],
        compiler_params=pltpu.CompilerParams(
            collective_id=0, has_side_effects=True, vmem_limit_bytes=VMEM
        ),
        name="channelize_and_exchange",
    )(samples, filter_taps, table)
    return pl.pallas_call(
        functools.partial(correlate_kernel, scale),
        out_shape=jax.ShapeDtypeStruct((2, chan_dev, all_inputs, all_inputs), jnp.float32),
        in_specs=[vmem, vmem, vmem],
        out_specs=hbm,
        scratch_shapes=[pltpu.VMEM(vis_shape, jnp.float32), pltpu.SemaphoreType.DMA],
        compiler_params=pltpu.CompilerParams(vmem_limit_bytes=VMEM // 2),
        name="correlate",
    )(early, late, vis)


def solution(mesh):
    devices = mesh.size
    table = dft_table(2048, devices)

    def whole(samples, filter_taps):
        return jax.shard_map(
            on_device,
            mesh=mesh,
            in_specs=(P(), P("inp", "tm"), P()),
            out_specs=P(None, ("inp", "tm"), None, None),
            check_vma=False,
        )(jnp.asarray(table), samples, filter_taps)

    return whole
```
